128 devices in a mesh: expert: 16 (over y, z), etp: 4 (over x), dp: 2 (over core).
Axes of the slice: x: 4, y: 4, z: 4, core: 2. Of those that a mesh axis runs over, the one named last changes fastest.
Arguments:
- out_grad: bfloat16 [8192, 3072], P(('expert', 'dp')), may hold values from -6 to 6
- route: int32 [8192, 4], P(('expert', 'dp')), may hold values from 0 to 15, all different within a row; in each aligned block of 256 rows (0 to 255, 256 to 511, ...) at most 96 rows name the same one
- gate_prob: bfloat16 [8192, 4], P(('expert', 'dp')), may hold values from 0.049804688 to 0.59765625
- w_down: bfloat16 [16, 5376, 3072], P('expert', 'etp'), may hold values from -0.078125 to 0.078125
- gate_pre: bfloat16 [16, 3072, 5376], P('expert', 'dp', 'etp'), may hold values from -6 to 6
- up_pre: bfloat16 [16, 3072, 5376], P('expert', 'dp', 'etp'), may hold values from -6 to 6
Outputs:
- grad_gate: bfloat16 [16, 3072, 5376], P('expert', 'dp', 'etp')
- grad_up: bfloat16 [16, 3072, 5376], P('expert', 'dp', 'etp')
- grad_down: bfloat16 [16, 5376, 3072], P('expert', ('etp', 'dp'))
- grad_prob: float32 [8192, 4], P(('expert', 'dp'))
The draws below stay inside these ranges and needn't reach their ends.
Inputs may be any that keep to these rules, and one draw needn't show every extreme that they name: `route`: each token names 4 different experts; among the 256 tokens of one device no expert is named more than 96 times, and in every draw some device names some expert exactly 96 times.
All inputs are finite; a program needn't handle non-finite values.
Results may differ from the reference program's by a relative error of at most 0.005.
Values may be sent and summed in bfloat16 or wider, within the bound.
No kernel may reach another device: no remote copies, remote signals or barrier semaphores. Data moves between devices by JAX's collectives and lax.ppermute only.
A program may use at most 192 MiB of HBM per device.

```python
import math
import jax
import jax.numpy as jnp
import numpy as np
from jax import lax

D = 3072
FF = 5376
TOP = 4
TOK_DEV = 256
EXPERTS = 16
CAP = 96
SLOTS = 1536
TOKENS = 8192
N_EXPERT = 16
N_DP = 2


def levels(stream_key, dims, split, least, largest):
    level = 1.0
    for axis_at, shards_of in split:
        heights = jax.random.uniform(jax.random.fold_in(jax.random.fold_in(stream_key, 6), axis_at), (shards_of,), jnp.float32, least / len(split), largest / len(split))
        level = level * jnp.repeat(jnp.exp(heights), dims[axis_at] // shards_of).reshape((-1,) + (1,) * (len(dims) - 1 - axis_at))
    return level


def deal_out(stream_key, own, number, rows, count, top, most, slope):
    ranking = jax.random.permutation(stream_key, count)
    crowded, usual = load_shares(count, rows * top, most, slope, True), load_shares(count, rows * top, most, slope, False)
    places = jnp.arange(count)

    def named(lengths, rotation):
        used = int((lengths > 0).sum())
        fixed = max(1, used // 4)
        moved = fixed + (places - fixed + rotation * (used - fixed)) % max(1, count - fixed)
        return jnp.zeros((count,), jnp.int32).at[ranking[jnp.where(places < fixed, places, moved)]].set(jnp.asarray(lengths, jnp.int32))

    lengths = jnp.where(number % 4 == 0, named(crowded, number // 4), named(usual, number - number // 4 - 1))
    mixed = jax.random.permutation(jax.random.fold_in(own, 3), count)
    giver, taker = mixed[0:count // 2 * 2:2], mixed[1:count // 2 * 2:2]
    margin = jnp.minimum(lengths[giver] - 1, most - lengths[taker]) // 2
    margin = jnp.where((giver == ranking[0]) | (taker == ranking[0]) | (lengths[taker] == 0), 0, jnp.maximum(margin, 0))
    moved = jax.random.randint(jax.random.fold_in(own, 4), (count // 2,), 0, 1 << 20) % (margin + 1)
    lengths = lengths.at[giver].add(-moved).at[taker].add(moved)
    members = jnp.searchsorted(jnp.cumsum(lengths), jnp.arange(rows * top), side="right").astype(jnp.int32)
    listing = members.reshape(top, rows).T
    listing = listing[jax.random.permutation(jax.random.fold_in(own, 1), rows)]
    rotation = jax.random.randint(jax.random.fold_in(own, 2), (rows, 1), 0, top)
    return jnp.take_along_axis(listing, (jnp.arange(top)[None, :] + rotation) % top, axis=1)


def load_shares(number_of, total, limit, lean, full):
    weights = [(1 << 20) // math.isqrt(grade ** lean) + 1 for grade in range(1, number_of + 1)]
    largest = limit if full else min(limit, max(-(-total // number_of), total * weights[0] // sum(weights)))
    least = 1 if total - largest >= number_of - 1 else 0
    holding, rest = [largest] + [least] * (number_of - 1), total - largest - least * (number_of - 1)
    while rest > 0:
        free = [i for i in range(1, number_of) if holding[i] < largest] or [i for i in range(1, number_of) if holding[i] < limit]
        pool, remaining = sum([weights[i] for i in free]), rest
        for i in free:
            addition = min(limit - holding[i], max(1, remaining * weights[i] // pool), rest)
            holding[i] = holding[i] + addition
            rest = rest - addition
    return np.array(holding)


def noise(rng, shape, deviation, bound, shards=(), kind=jnp.bfloat16):
    drawn = jax.random.normal(rng, shape, jnp.float32) * deviation
    if len(shards) > 0:
        drawn = levels(rng, shape, shards, -0.22, 0.18) * drawn
    return jnp.clip(drawn, min=-bound, max=bound).astype(kind)


def setup_inputs(seed: int = 0) -> dict:
    keys = jax.random.split(jax.random.key(seed), 7)
    out_grad = noise(keys[0], (TOKENS, D), 1.0, 6.0, ((0, 32),))
    route_keys = jax.random.split(jax.random.fold_in(keys[1], 1), TOKENS // TOK_DEV)
    route_turns = jax.random.permutation(jax.random.fold_in(keys[1], 3), TOKENS // TOK_DEV)
    route = jax.vmap(lambda own, number: deal_out(jax.random.fold_in(keys[1], 2), own, number, TOK_DEV, EXPERTS, TOP, CAP, 2))(route_keys, route_turns).reshape((TOKENS, TOP))
    gate_prob = jnp.clip(jnp.exp(math.log(0.59765625) - 2.4849066 * jax.random.uniform(keys[2], (TOKENS, TOP), jnp.float32) ** levels(keys[2], (TOKENS, TOP), ((0, 32),), -0.2, 0.2)), 0.049804688, 0.59765625).astype(jnp.bfloat16)
    w_down = noise(keys[3], (EXPERTS, FF, D), FF ** -0.5, 0.078125, ((0, 16), (1, 4)))
    gate_pre = noise(keys[4], (EXPERTS, N_DP * SLOTS, FF), 1.0, 6.0, ((0, 16), (1, 2), (2, 4)))
    up_pre = noise(keys[5], (EXPERTS, N_DP * SLOTS, FF), 1.0, 6.0, ((0, 16), (1, 2), (2, 4)))
    return dict(out_grad=out_grad, route=route, gate_prob=gate_prob, w_down=w_down, gate_pre=gate_pre, up_pre=up_pre)


def reference(out_grad, route, gate_prob, w_down, gate_pre, up_pre):
    blocks = N_EXPERT * N_DP
    total_slots = N_DP * SLOTS
    grouped = route.reshape(blocks, TOK_DEV * TOP)
    onehot = (grouped[:, :, None] == jnp.arange(EXPERTS, dtype=jnp.int32)[None, None, :]).astype(jnp.int32)
    before = jnp.cumsum(onehot, axis=1) - onehot
    position = jnp.sum(before * onehot, axis=2)
    block_ids = jnp.arange(blocks, dtype=jnp.int32)
    source = block_ids // N_DP
    replica = block_ids % N_DP
    target = (replica[:, None] * SLOTS + source[:, None] * CAP + position).astype(jnp.int32)
    target = target.reshape(TOKENS, TOP)

    def one_expert(expert_id):
        rows = jnp.zeros((total_slots, D), jnp.bfloat16)
        weight = jnp.zeros((total_slots,), jnp.bfloat16)
        for choice_k in range(TOP):
            index = jnp.where(route[:, choice_k] == expert_id, target[:, choice_k], total_slots).astype(jnp.int32)
            rows = rows.at[index].set(out_grad, mode="drop")
            weight = weight.at[index].set(gate_prob[:, choice_k], mode="drop")
        w_local = lax.dynamic_index_in_dim(w_down, expert_id, 0, keepdims=False)
        gate = lax.dynamic_index_in_dim(gate_pre, expert_id, 0, keepdims=False).astype(jnp.float32)
        upper = lax.dynamic_index_in_dim(up_pre, expert_id, 0, keepdims=False).astype(jnp.float32)
        raw = lax.dot_general(rows, w_local, (((1,), (1,)), ((), ())), preferred_element_type=jnp.float32)
        sig = jax.nn.sigmoid(gate)
        act = gate * sig * upper
        prob = weight.astype(jnp.float32)[:, None]
        scaled_grad = prob * raw
        grad_up = (scaled_grad * (gate * sig)).astype(jnp.bfloat16)
        grad_gate = (scaled_grad * upper * (sig * (1.0 + gate * (1.0 - sig)))).astype(jnp.bfloat16)
        scaled = (prob * act).astype(jnp.bfloat16)
        grad_down = lax.dot_general(scaled, rows, (((0,), (0,)), ((), ())), preferred_element_type=jnp.float32).astype(jnp.bfloat16)
        slot_prob = jnp.sum(raw * act, axis=1)
        return grad_gate, grad_up, grad_down, slot_prob

    grad_gate, grad_up, grad_down, slot_prob = lax.map(one_expert, jnp.arange(EXPERTS, dtype=jnp.int32))
    grad_prob = slot_prob[route, target]
    return grad_gate, grad_up, grad_down, grad_prob
```

```python
import functools

import jax
import jax.numpy as jnp
from jax import lax
from jax.experimental import pallas as pl
from jax.experimental.pallas import tpu as pltpu
from jax.sharding import PartitionSpec as P

BF16 = jnp.bfloat16
F32 = jnp.float32
LANES = 128
CHUNKS = ((0, 32), (32, 32), (64, 32))
TILE_FF = 256
TILE_D = 512


def params(megabytes):
    return pltpu.CompilerParams(
        dimension_semantics=("arbitrary",), vmem_limit_bytes=megabytes << 20
    )


def cost(flops, moved):
    return pl.CostEstimate(flops=flops, bytes_accessed=moved, transcendentals=0)


def dispatch_kernel(experts, chunks, where_ref, route_ref, prob_ref, grad_ref, *refs):
    outs, slot_ref, pick = refs[: len(chunks)], refs[len(chunks)], refs[len(chunks) + 1]
    tokens = route_ref.shape[0]
    half = grad_ref.shape[1]
    expert = lax.broadcasted_iota(jnp.int32, (tokens, LANES), 1)
    chosen = jnp.zeros((tokens, LANES), F32)
    prob = jnp.zeros((tokens, LANES), F32)
    for k in range(route_ref.shape[1]):
        hit = route_ref[:, k : k + 1] == expert
        chosen = jnp.where(hit, 1.0, chosen)
        prob = jnp.where(hit, prob_ref[:, k : k + 1].astype(F32), prob)
    chosen = chosen.astype(BF16)
    row = lax.broadcasted_iota(jnp.int32, (tokens, tokens), 0)
    col = lax.broadcasted_iota(jnp.int32, (tokens, tokens), 1)
    earlier = (row < col).astype(BF16)
    same = (row == col).astype(BF16)
    lower = (col < row).astype(BF16)
    over_rows = (((0,), (0,)), ((), ()))
    before_t = lax.dot_general(chosen, earlier, over_rows, preferred_element_type=F32)
    chosen_t = lax.dot_general(chosen, same, over_rows, preferred_element_type=F32)
    slot_t = jnp.where(chosen_t > 0.5, before_t, -1.0)
    slot_ref[...] = jnp.dot(lower, chosen, preferred_element_type=F32)
    prob = prob.astype(BF16)
    for (start, rows), out in zip(chunks, outs):
        place = lax.broadcasted_iota(jnp.int32, (rows, tokens), 0).astype(F32) + float(start)
        for e in range(experts):
            pick[pl.ds(e * rows, rows), :] = (slot_t[e : e + 1, :] == place).astype(BF16)
        chosen_rows = pick[pl.ds(0, experts * rows), :]
        out[:, :half] = jnp.dot(
            chosen_rows, grad_ref[...], preferred_element_type=F32
        ).astype(BF16)
        out[:, half:] = jnp.dot(chosen_rows, prob, preferred_element_type=F32).astype(BF16)


def dispatch(where, route, prob, grad, experts, chunks):
    tokens, width = grad.shape
    half = width // 2
    wide = half + LANES
    total = sum(rows for _, rows in chunks) * experts
    most = max(rows for _, rows in chunks) * experts
    return pl.pallas_call(
        functools.partial(dispatch_kernel, experts, chunks),
        out_shape=[jax.ShapeDtypeStruct((experts * r, wide), BF16) for _, r in chunks]
        + [jax.ShapeDtypeStruct((tokens, LANES), F32)],
        grid_spec=pltpu.PrefetchScalarGridSpec(
            num_scalar_prefetch=1,
            grid=(1,),
            in_specs=[
                pl.BlockSpec(route.shape, lambda i, w: (0, 0)),
                pl.BlockSpec(prob.shape, lambda i, w: (0, 0)),
                pl.BlockSpec((tokens, half), lambda i, w: (0, w[0])),
            ],
            out_specs=[pl.BlockSpec((experts * r, wide), lambda i, w: (0, 0)) for _, r in chunks]
            + [pl.BlockSpec((tokens, LANES), lambda i, w: (0, 0))],
            scratch_shapes=[pltpu.VMEM((most, tokens), BF16)],
        ),
        compiler_params=params(24),
        cost_estimate=cost(2 * total * tokens * wide, 2 * (tokens * half + total * wide)),
        name="dispatch",
    )(where, route, prob, grad)


def hidden_kernel(ff, first, where_ref, own_ref, oth_ref, wown_ref, woth_ref, gate_ref, up_ref, *refs):
    gg_ref, gu_ref, sct_ref, part_ref, acc = refs if first else refs[2:]
    n = pl.program_id(0)
    groups, rows, _ = gate_ref.shape
    tile = gate_ref.shape[2]
    half = oth_ref.shape[2] - LANES
    lane = lax.broadcasted_iota(jnp.int32, (1, LANES), 1)
    valid = lax.broadcasted_iota(jnp.int32, (1, tile), 1) + n * tile < ff
    by_col = (((1,), (1,)), ((), ()))

    @pl.when(n == 0)
    def _():
        acc[...] = jnp.zeros_like(acc)

    step = max(1, 128 // rows)
    for g in range(0, groups, step):
        size = step * rows
        own = own_ref[g : g + step].reshape(size, half + LANES)
        oth = oth_ref[g : g + step].reshape(size, half + LANES)
        raw = lax.dot_general(own[:, :half], wown_ref[...], by_col, preferred_element_type=F32)
        raw += lax.dot_general(oth[:, :half], woth_ref[...], by_col, preferred_element_type=F32)
        weight = jnp.sum(
            jnp.where(lane == where_ref[1], own[:, half:].astype(F32), 0.0), axis=1, keepdims=True
        )
        gate = gate_ref[g : g + step].reshape(size, tile).astype(F32)
        upper = up_ref[g : g + step].reshape(size, tile).astype(F32)
        sig = 0.5 * jnp.tanh(0.5 * gate) + 0.5
        gs = gate * sig
        act = gs * upper
        scaled_grad = weight * raw
        gu_ref[g : g + step] = (scaled_grad * gs).astype(BF16).reshape(step, rows, tile)
        gg_ref[g : g + step] = (
            (scaled_grad * upper * (sig + gs * (1.0 - sig))).astype(BF16).reshape(step, rows, tile)
        )
        sct_ref[:, g * rows : g * rows + size] = (weight * act).astype(BF16).T
        term = jnp.where(valid, raw * act, 0.0)
        total = term[:, :LANES]
        for at in range(LANES, tile, LANES):
            total += term[:, at : at + LANES]
        acc[g * rows : g * rows + size, :] += total

    @pl.when(n == pl.num_programs(0) - 1)
    def _():
        part_ref[...] = jnp.sum(acc[...].reshape(groups, rows, LANES), axis=2)


def hidden(where, own, oth, w, gate, up, before, chunk):
    start, rows = chunk
    groups, capacity, ff = gate.shape
    width = w.shape[1]
    half = width // 2
    size = groups * rows
    at = start // rows
    block = (groups, rows, TILE_FF)
    spec = pl.BlockSpec(block, lambda n, s: (0, at, n))
    whole = pl.BlockSpec(own.shape, lambda n, s: (0, 0, 0))
    first = before is None
    return pl.pallas_call(
        functools.partial(hidden_kernel, ff, first),
        out_shape=[
            jax.ShapeDtypeStruct(gate.shape, BF16),
            jax.ShapeDtypeStruct(gate.shape, BF16),
            jax.ShapeDtypeStruct((ff, size), BF16),
            jax.ShapeDtypeStruct((groups, rows), F32),
        ],
        grid_spec=pltpu.PrefetchScalarGridSpec(
            num_scalar_prefetch=1,
            grid=(pl.cdiv(ff, TILE_FF),),
            in_specs=[
                whole,
                whole,
                pl.BlockSpec((TILE_FF, half), lambda n, s: (n, s[0])),
                pl.BlockSpec((TILE_FF, half), lambda n, s: (n, 1 - s[0])),
                spec,
                spec,
            ]
            + ([] if first else [pl.BlockSpec(memory_space=pl.ANY)] * 2),
            out_specs=[
                spec,
                spec,
                pl.BlockSpec((TILE_FF, size), lambda n, s: (n, 0)),
                pl.BlockSpec((groups, rows), lambda n, s: (0, 0)),
            ],
            scratch_shapes=[pltpu.VMEM((size, LANES), F32)],
        ),
        input_output_aliases={} if first else {7: 0, 8: 1},
        compiler_params=params(32),
        cost_estimate=cost(2 * size * ff * width, 2 * (ff * width + size * width + 5 * size * ff)),
        name="hidden",
    )(where, own, oth, w, w, gate, up, *(() if first else before))


def down_kernel(count, fused, where_ref, *refs):
    total = jnp.dot(refs[0][...], refs[count][...], preferred_element_type=F32)
    for c in range(1, count):
        total += jnp.dot(refs[c][...], refs[count + c][...], preferred_element_type=F32)
    if fused:
        total += refs[2 * count][...].astype(F32)
    refs[-1][...] = total.astype(BF16)


def down(where, scaled, rows, mine, own_cols, got=None, into=None):
    count = len(scaled)
    ff = scaled[0].shape[0]
    half_ff = ff // 2
    wide = rows[0].shape[1]
    half = wide - LANES
    tiles = half // TILE_D
    fused = got is not None
    pick = (lambda i, s: (s[2], 0)) if mine else (lambda i, s: (1 - s[2], 0))
    in_specs = [pl.BlockSpec((half_ff, s.shape[1]), pick) for s in scaled]
    in_specs += [pl.BlockSpec((r.shape[0], TILE_D), lambda i, s: (0, i)) for r in rows]
    args = [where, *scaled, *rows]
    aliases = {}
    if fused:
        in_specs.append(pl.BlockSpec((half_ff, TILE_D), lambda i, s: (0, i)))
        args.append(got)
        if own_cols:
            out_spec = pl.BlockSpec((half_ff, TILE_D), lambda i, s: (0, s[0] * tiles + i))
        else:
            out_spec = pl.BlockSpec((half_ff, TILE_D), lambda i, s: (0, (1 - s[0]) * tiles + i))
        if into is not None:
            in_specs.append(pl.BlockSpec(memory_space=pl.ANY))
            aliases = {len(args): 0}
            args.append(into)
        out_cols = 2 * half
    else:
        out_spec = pl.BlockSpec((half_ff, TILE_D), lambda i, s: (0, i))
        out_cols = half
    depth = sum(s.shape[1] for s in scaled)
    return pl.pallas_call(
        functools.partial(down_kernel, count, fused),
        out_shape=jax.ShapeDtypeStruct((half_ff, out_cols), BF16),
        grid_spec=pltpu.PrefetchScalarGridSpec(
            num_scalar_prefetch=1, grid=(tiles,), in_specs=in_specs, out_specs=out_spec
        ),
        input_output_aliases=aliases,
        compiler_params=params(32),
        cost_estimate=cost(
            2 * half_ff * half * depth, 2 * (half_ff * half * 2 + depth * (half + half_ff))
        ),
        name="down",
    )(*args)


def combine_kernel(experts, route_ref, slot_ref, *refs):
    out_ref = refs[-1]
    values = refs[0][...]
    for ref in refs[1:-1]:
        values += ref[...]
    tokens = route_ref.shape[0]
    capacity = values.shape[1]
    place = lax.broadcasted_iota(jnp.int32, (tokens, capacity), 1).astype(F32)
    route = route_ref[...]
    total = jnp.zeros(route.shape, F32)
    for e in range(experts):
        hit = slot_ref[:, e : e + 1] == place
        mine = jnp.sum(jnp.where(hit, values[e : e + 1, :], 0.0), axis=1, keepdims=True)
        total = jnp.where(route == e, mine, total)
    out_ref[...] = total


def combine(route, slot, values):
    experts = values[0].shape[0]
    return pl.pallas_call(
        functools.partial(combine_kernel, experts),
        out_shape=jax.ShapeDtypeStruct(route.shape, F32),
        name="combine",
    )(route, slot, *values)


def local(out_grad, route, gate_prob, w_down, gate_pre, up_pre):
    experts = lax.axis_size("expert")
    etp = lax.axis_size("etp")
    slots, ff = gate_pre.shape[1:]
    capacity = slots // experts
    width = out_grad.shape[1]
    half = width // 2
    wide = half + LANES
    where = jnp.stack(
        [lax.axis_index("etp") % 2, lax.axis_index("expert"), lax.axis_index("dp")]
    ).astype(jnp.int32)
    *sends, slot = dispatch(where, route, gate_prob, out_grad, experts, CHUNKS)
    swap = [(2 * i, 2 * ((i - 1) % etp)) for i in range(etp)]
    swap += [(2 * i + 1, 2 * ((i + 1) % etp) + 1) for i in range(etp)]
    gate = gate_pre.reshape(experts, capacity, ff)
    up = up_pre.reshape(experts, capacity, ff)
    before = None
    own_rows, oth_rows, scaled, parts = [], [], [], []
    for chunk, send in zip(CHUNKS, sends):
        rows = chunk[1]
        own = lax.all_to_all(
            send.reshape(experts, rows, wide), "expert", split_axis=0, concat_axis=0, tiled=True
        )
        oth = lax.ppermute(own, ("etp", "dp"), swap)
        *before, sct, part = hidden(where, own, oth, w_down[0], gate, up, before, chunk)
        own_rows.append(own.reshape(experts * rows, wide))
        oth_rows.append(oth.reshape(experts * rows, wide))
        scaled.append(sct)
        parts.append(part)
    partial_sum = jnp.concatenate(parts, axis=1)
    back = lax.all_to_all(partial_sum, "expert", split_axis=0, concat_axis=0, tiled=True)
    others = [
        lax.ppermute(back, "etp", [(i, (i + k) % etp) for i in range(etp)]) for k in range(1, etp)
    ]
    other = [(0, 1), (1, 0)]
    got_own = lax.ppermute(down(where, scaled, own_rows, False, True), "dp", other)
    got_oth = lax.ppermute(down(where, scaled, oth_rows, False, False), "dp", other)
    grad_down = down(where, scaled, own_rows, True, True, got_own)
    grad_down = down(where, scaled, oth_rows, True, False, got_oth, grad_down)
    grad_prob = combine(route, slot, [back, *others])
    grad_gate, grad_up = before
    return (
        grad_gate.reshape(gate_pre.shape),
        grad_up.reshape(up_pre.shape),
        grad_down[None],
        grad_prob,
    )


def solution(mesh):
    in_specs = (
        P(("expert", "dp"), None),
        P(("expert", "dp"), None),
        P(("expert", "dp"), None),
        P("expert", "etp", None),
        P("expert", "dp", "etp"),
        P("expert", "dp", "etp"),
    )
    out_specs = (
        P("expert", "dp", "etp"),
        P("expert", "dp", "etp"),
        P("expert", ("etp", "dp"), None),
        P(("expert", "dp"), None),
    )
    return jax.shard_map(local, mesh=mesh, in_specs=in_specs, out_specs=out_specs, check_vma=False)
```

```python
import functools

import jax
import jax.numpy as jnp
from jax import lax
from jax.experimental import pallas as pl
from jax.experimental.pallas import tpu as pltpu
from jax.sharding import PartitionSpec as P

BF16 = jnp.bfloat16
F32 = jnp.float32
LANES = 128
SHARED = ((0, 768), (1536, 512))
DIRECT = (2560, 512)
TILE_FF = 336
TILE_D = 256
SUB = 16
COLS = 256
VMEM_MB = 56
NT = (((1,), (1,)), ((), ()))


def params():
    return pltpu.CompilerParams(
        dimension_semantics=("arbitrary",), vmem_limit_bytes=VMEM_MB << 20
    )


def cost(flops, moved):
    flops, moved = flops // 4, moved // 4
    return pl.CostEstimate(flops=flops, bytes_accessed=moved, transcendentals=0)


def call(kernel, name, grid, in_specs, out_specs, out_shape, scratch, flops, moved, aliases=None):
    return pl.pallas_call(
        kernel,
        out_shape=out_shape,
        grid_spec=pltpu.PrefetchScalarGridSpec(
            num_scalar_prefetch=1,
            grid=grid,
            in_specs=in_specs,
            out_specs=out_specs,
            scratch_shapes=scratch,
        ),
        input_output_aliases=aliases or {},
        compiler_params=params(),
        cost_estimate=cost(flops, moved),
        name=name,
    )


def fixed(i, s):
    return (0, 0)


OWN, OTHER, SAME = 0, 1, 2


def column(chunk, side):
    first, size = chunk
    if side == SAME:
        return lambda s: first // size
    return lambda s: first // size + (s[0] if side == OWN else 1 - s[0])


def dispatch_kernel(experts, capacity, where_ref, route_ref, prob_ref, grad_ref,
                    send_ref, slot_ref, pick_ref):
    top, tokens = route_ref.shape
    expert = lax.broadcasted_iota(jnp.int32, (experts, tokens), 0)
    chosen = jnp.zeros((experts, tokens), F32)
    prob = jnp.zeros((experts, tokens), F32)
    for k in range(top):
        hit = route_ref[k : k + 1, :] == expert
        chosen = jnp.where(hit, 1.0, chosen)
        prob = jnp.where(hit, prob_ref[k : k + 1, :].astype(F32), prob)
    row = lax.broadcasted_iota(jnp.int32, (tokens, tokens), 0)
    col = lax.broadcasted_iota(jnp.int32, (tokens, tokens), 1)
    earlier = (row < col).astype(BF16)
    before = jnp.dot(chosen.astype(BF16), earlier, preferred_element_type=F32)
    slot = jnp.where(chosen > 0.5, before, -1.0)
    slot_ref[...] = slot
    place = lax.broadcasted_iota(jnp.int32, (capacity, tokens), 0).astype(F32)
    for e in range(experts):
        pick_ref[pl.ds(e * capacity, capacity), :] = jnp.where(
            slot[e : e + 1, :] == place, prob[e : e + 1, :], 0.0
        ).astype(BF16)
    send_ref[...] = jnp.dot(
        pick_ref[...], grad_ref[...], preferred_element_type=F32
    ).astype(BF16)


def dispatch(where, route, prob, grad, experts, capacity):
    tokens, width = grad.shape
    at = column(SHARED[0], OWN)
    part = SHARED[0][1]
    total = experts * capacity
    return call(
        functools.partial(dispatch_kernel, experts, capacity),
        "dispatch",
        (1,),
        [
            pl.BlockSpec(route.shape, fixed),
            pl.BlockSpec(prob.shape, fixed),
            pl.BlockSpec((tokens, part), lambda i, s: (0, at(s))),
        ],
        [
            pl.BlockSpec((total, part), fixed),
            pl.BlockSpec((experts, tokens), fixed),
            pl.BlockSpec((total, tokens), fixed),
        ],
        [
            jax.ShapeDtypeStruct((total, part), BF16),
            jax.ShapeDtypeStruct((experts, tokens), F32),
            jax.ShapeDtypeStruct((total, tokens), BF16),
        ],
        [],
        2 * total * tokens * part,
        2 * total * part,
    )(where, route, prob, grad)


def more_kernel(where_ref, pick_ref, grad_ref, send_ref):
    send_ref[...] = jnp.dot(
        pick_ref[...], grad_ref[...], preferred_element_type=F32
    ).astype(BF16)


def dispatch_more(where, pick, grad, chunk, side):
    total, tokens = pick.shape
    part = chunk[1]
    at = column(chunk, side)
    return call(
        more_kernel,
        "dispatch_more",
        (2,),
        [
            pl.BlockSpec((total // 2, tokens), lambda i, s: (i, 0)),
            pl.BlockSpec((tokens, part), lambda i, s: (0, at(s))),
        ],
        pl.BlockSpec((total // 2, part), lambda i, s: (i, 0)),
        jax.ShapeDtypeStruct((total, part), BF16),
        [],
        2 * total * tokens * part,
        2 * total * part,
    )(where, pick, grad)


def over_blocks(shape, body):
    def step(i, _):
        at = pl.ds(pl.multiple_of(i * SUB, SUB), SUB)
        for c in range(0, shape[1], COLS):
            body(at, pl.ds(c, COLS))
        return 0

    lax.fori_loop(0, shape[0] // SUB, step, 0)


def act_kernel(where_ref, gate_ref, up_ref, other_ref, mine_ref):
    def fill(out_ref):
        def body(at, cols):
            gate = gate_ref[at, cols].astype(F32)
            sig = 0.5 * jnp.tanh(0.5 * gate) + 0.5
            out_ref[at, cols] = (gate * sig * up_ref[at, cols].astype(F32)).astype(BF16)

        over_blocks(gate_ref.shape, body)

    @pl.when(pl.program_id(0) == 0)
    def _():
        fill(other_ref)

    @pl.when(pl.program_id(0) == 1)
    def _():
        fill(mine_ref)


def activation(where, gate, up):
    ff, slots = gate.shape
    tiles = ff // 2 // TILE_FF
    side = lambda h, s: h * s[2] + (1 - h) * (1 - s[2])
    spec = pl.BlockSpec((TILE_FF, slots), lambda h, n, s: (side(h, s) * tiles + n, 0))
    out = jax.ShapeDtypeStruct((ff // 2, slots), BF16)
    return pl.pallas_call(
        act_kernel,
        out_shape=[out, out],
        grid_spec=pltpu.PrefetchScalarGridSpec(
            num_scalar_prefetch=1,
            grid=(2, tiles),
            in_specs=[spec, spec],
            out_specs=[
                pl.BlockSpec((TILE_FF, slots), lambda h, n, s: (jnp.where(h == 0, n, tiles - 1), 0)),
                pl.BlockSpec((TILE_FF, slots), lambda h, n, s: (jnp.where(h == 0, 0, n), 0)),
            ],
        ),
        compiler_params=pltpu.CompilerParams(
            dimension_semantics=("arbitrary", "arbitrary"), vmem_limit_bytes=VMEM_MB << 20
        ),
        cost_estimate=cost(20 * ff * slots, 6 * ff * slots),
        name="activation",
    )(where, gate, up)


def piece_specs(pieces, slots):
    specs = []
    for _, chunk, side in pieces:
        at = column(chunk, side)
        specs.append(pl.BlockSpec((slots, chunk[1]), fixed))
        specs.append(pl.BlockSpec((TILE_FF, chunk[1]), lambda n, s, at=at: (n, at(s))))
    return specs


def piece_dots(refs, count):
    total = None
    for p in range(count):
        term = lax.dot_general(
            refs[2 * p + 1][...], refs[2 * p][...], NT, preferred_element_type=F32
        )
        total = term if total is None else total + term
    return total


def raw_kernel(count, more, where_ref, *refs):
    total = piece_dots(refs, count)
    if more:
        total += refs[2 * count][...]
    refs[-1][...] = total


def raw_part(where, w, pieces, before=None):
    slots = pieces[0][0].shape[0]
    ff, width = w.shape
    depth = sum(chunk[1] for _, chunk, _ in pieces)
    tile = pl.BlockSpec((TILE_FF, slots), lambda n, s: (n, 0))
    args = [x for rows, _, _ in pieces for x in (rows, w)]
    more = before is not None
    return call(
        functools.partial(raw_kernel, len(pieces), more),
        "raw",
        (ff // TILE_FF,),
        piece_specs(pieces, slots) + ([tile] if more else []),
        tile,
        jax.ShapeDtypeStruct((ff, slots), F32),
        [],
        2 * slots * ff * depth,
        2 * (ff + slots) * depth + 8 * ff * slots,
    )(where, *args, *([before] if more else []))


def finish_kernel(count, where_ref, gate_ref, up_ref, before_ref, *refs):
    gg_ref, gu_ref, part_ref, acc = refs[2 * count :]
    tile, slots = gate_ref.shape

    @pl.when(pl.program_id(0) == 0)
    def _():
        acc[...] = jnp.zeros_like(acc)

    for c in range(0, slots, COLS):
        cols = pl.ds(c, COLS)
        raw = before_ref[:, cols]
        for p in range(count):
            raw += lax.dot_general(
                refs[2 * p + 1][...], refs[2 * p][cols, :], NT, preferred_element_type=F32
            )
        total = jnp.zeros((8, COLS), F32)
        for r in range(0, tile, SUB):
            at = pl.ds(r, SUB)
            gate = gate_ref[at, cols].astype(F32)
            upper = up_ref[at, cols].astype(F32)
            value = raw[r : r + SUB]
            sig = 0.5 * jnp.tanh(0.5 * gate) + 0.5
            gs = gate * sig
            gu_ref[at, cols] = (value * gs).astype(BF16)
            gg_ref[at, cols] = (value * upper * (sig + gs * (1.0 - sig))).astype(BF16)
            term = value * (gs * upper)
            total += term[:8] + term[8:]
        acc[:, cols] += total

    @pl.when(pl.program_id(0) == pl.num_programs(0) - 1)
    def _():
        total = jnp.sum(acc[...], axis=0, keepdims=True)
        groups, capacity = part_ref.shape
        for g in range(groups):
            part_ref[g : g + 1, :] = total[:, g * capacity : (g + 1) * capacity]


def finish(where, gate, up, before, w, pieces, groups):
    ff, slots = gate.shape
    depth = sum(chunk[1] for _, chunk, _ in pieces)
    tile = pl.BlockSpec((TILE_FF, slots), lambda n, s: (n, 0))
    args = [x for rows, _, _ in pieces for x in (rows, w)]
    return call(
        functools.partial(finish_kernel, len(pieces)),
        "finish",
        (ff // TILE_FF,),
        [tile, tile, tile] + piece_specs(pieces, slots),
        [tile, tile, pl.BlockSpec((groups, slots // groups), fixed)],
        [
            jax.ShapeDtypeStruct((ff, slots), BF16),
            jax.ShapeDtypeStruct((ff, slots), BF16),
            jax.ShapeDtypeStruct((groups, slots // groups), F32),
        ],
        [pltpu.VMEM((8, slots), F32)],
        2 * slots * ff * depth,
        2 * (ff + slots) * depth + 12 * ff * slots,
    )(where, gate, up, before, *args)


def down_kernel(counts, where_ref, here_ref, there_ref, *refs):
    at = 0
    for p, count in enumerate(counts):

        @pl.when((pl.program_id(0) >= at) & (pl.program_id(0) < at + count))
        def _(p=p):
            total = jnp.dot(here_ref[...], refs[2 * p][...], preferred_element_type=F32)
            total += jnp.dot(there_ref[...], refs[2 * p + 1][...], preferred_element_type=F32)
            refs[-1][...] = total.astype(BF16)

        at += count


def down(where, acts, pieces, width, into=None):
    half_ff, slots = acts[0].shape
    counts = [chunk[1] // TILE_D for _, _, chunk, _ in pieces]
    tiles = sum(counts)
    in_specs = [pl.BlockSpec((half_ff, slots), fixed)] * 2
    args = [where, *acts]
    starts = []
    for p, (here, there, _, _) in enumerate(pieces):
        start = sum(counts[:p])
        starts.append(start)
        place = lambda i, s, a=start, n=counts[p]: (0, jnp.clip(i - a, 0, n - 1))
        in_specs += [pl.BlockSpec((slots, TILE_D), place)] * 2
        args += [here, there]

    def place_out(i, s):
        at = 0
        for (_, _, chunk, side), start, count in zip(pieces, starts, counts):
            first = column(chunk, side)(s) * count
            at = jnp.where((i >= start) & (i < start + count), first + i - start, at)
        return (0, at)

    aliases = {}
    if into is not None:
        in_specs.append(pl.BlockSpec(memory_space=pl.ANY))
        aliases = {len(args): 0}
        args.append(into)
    return call(
        functools.partial(down_kernel, counts),
        "down",
        (tiles,),
        in_specs,
        pl.BlockSpec((half_ff, TILE_D), place_out),
        jax.ShapeDtypeStruct((half_ff, width), BF16),
        [],
        4 * half_ff * TILE_D * slots * tiles,
        2 * (half_ff * TILE_D + 2 * slots * TILE_D) * tiles + 4 * slots * half_ff,
        aliases,
    )(*args)


def combine_kernel(experts, route_ref, prob_ref, slot_ref, *refs):
    out_ref = refs[-1]
    values = refs[0][...]
    for ref in refs[1:-1]:
        values += ref[...]
    capacity = values.shape[1]
    tokens = route_ref.shape[1]
    columns = values.T
    place = lax.broadcasted_iota(jnp.int32, (capacity, tokens), 0).astype(F32)
    route = route_ref[...]
    total = jnp.zeros(route.shape, F32)
    for e in range(experts):
        hit = slot_ref[e : e + 1, :] == place
        mine = jnp.sum(jnp.where(hit, columns[:, e : e + 1], 0.0), axis=0, keepdims=True)
        total = jnp.where(route == e, mine, total)
    out_ref[...] = total / prob_ref[...].astype(F32)


def combine(route, prob, slot, values):
    experts = values[0].shape[0]
    return pl.pallas_call(
        functools.partial(combine_kernel, experts),
        out_shape=jax.ShapeDtypeStruct(route.shape, F32),
        name="combine",
    )(route, prob, slot, *values)


def local(out_grad, route, gate_prob, w_down, gate_pre, up_pre):
    experts = lax.axis_size("expert")
    etp = lax.axis_size("etp")
    slots, ff = gate_pre.shape[1:]
    capacity = slots // experts
    width = out_grad.shape[1]
    where = jnp.stack(
        [lax.axis_index("etp") % 2, lax.axis_index("expert"), lax.axis_index("dp")]
    ).astype(jnp.int32)
    gate, up, w = gate_pre[0].T, up_pre[0].T, w_down[0]
    route, prob = route.T, gate_prob.T

    swap = [(2 * i, 2 * ((i - 1) % etp)) for i in range(etp)]
    swap += [(2 * i + 1, 2 * ((i + 1) % etp) + 1) for i in range(etp)]

    def fetch(send):
        x = send.reshape(experts, capacity, send.shape[1])
        x = lax.all_to_all(x, "expert", split_axis=0, concat_axis=0, tiled=True)
        return x.reshape(send.shape)

    def beside(x):
        return lax.ppermute(x, ("etp", "dp"), swap)

    def swap_dp(x):
        return lax.ppermute(x, "dp", [(0, 1), (1, 0)])

    c0, c1 = SHARED
    first, slot, pick = dispatch(where, route, prob, out_grad, experts, capacity)
    own0 = fetch(first)
    send1 = dispatch_more(where, pick, out_grad, c1, OWN)
    send2 = dispatch_more(where, pick, out_grad, DIRECT, SAME)
    act_other, act_mine = activation(where, gate, up)
    acts = (act_mine, swap_dp(act_other))
    own0, send1, send2, acts = lax.optimization_barrier((own0, send1, send2, acts))
    own1 = fetch(send1)
    oth0 = beside(own0)
    total = down(where, acts, [(own0, swap_dp(own0), c0, OWN)], width)
    own1, send2, total = lax.optimization_barrier((own1, send2, total))
    direct = fetch(send2)
    own1, oth0 = lax.optimization_barrier((own1, oth0))
    oth1 = beside(own1)
    raw = raw_part(where, w, [(own0, c0, OWN), (own1, c1, OWN), (oth0, c0, OTHER)])
    direct, oth1, raw = lax.optimization_barrier((direct, oth1, raw))
    late = [(oth1, c1, OTHER), (direct, DIRECT, SAME)]
    grad_gate, grad_up, sums = finish(where, gate, up, raw, w, late, experts)
    back = lax.all_to_all(sums, "expert", split_axis=0, concat_axis=0, tiled=True)
    pieces = [(own1, c1, OWN), (oth0, c0, OTHER)] + late
    pieces = [(rows, swap_dp(rows), chunk, side) for rows, chunk, side in pieces]
    total = down(where, acts, pieces, width, total)
    back, total = lax.optimization_barrier((back, total))
    others = [
        lax.ppermute(back, "etp", [(i, (i + k) % etp) for i in range(etp)]) for k in range(1, etp)
    ]
    grad_prob = combine(route, prob, slot, [back, *others])
    return grad_gate.T[None], grad_up.T[None], total[None], grad_prob.T


def solution(mesh):
    in_specs = (
        P(("expert", "dp"), None),
        P(("expert", "dp"), None),
        P(("expert", "dp"), None),
        P("expert", "etp", None),
        P("expert", "dp", "etp"),
        P("expert", "dp", "etp"),
    )
    out_specs = (
        P("expert", "dp", "etp"),
        P("expert", "dp", "etp"),
        P("expert", ("etp", "dp"), None),
        P(("expert", "dp"), None),
    )
    return jax.shard_map(local, mesh=mesh, in_specs=in_specs, out_specs=out_specs, check_vma=False)
```

```python
import functools

import jax
import jax.numpy as jnp
from jax import lax
from jax.experimental import pallas as pl
from jax.experimental.pallas import tpu as pltpu
from jax.sharding import PartitionSpec as P

BF16 = jnp.bfloat16
F32 = jnp.float32
LANES = 128
SHARED = ((0, 512), (1536, 768))
DIRECT = (1024, 512)
TILE_FF = 336
TILE_D = 256
SUB = 16
COLS = 256
VMEM_MB = {"dispatch": 16, "dispatch_more": 12, "activation": 16, "raw": 56, "finish": 56, "down": 20}
NT = (((1,), (1,)), ((), ()))


def params(name):
    return pltpu.CompilerParams(
        dimension_semantics=("arbitrary",), vmem_limit_bytes=VMEM_MB[name] << 20
    )


def cost(flops, moved):
    flops, moved = flops // 4, moved // 4
    return pl.CostEstimate(flops=flops, bytes_accessed=moved, transcendentals=0)


def call(kernel, name, grid, in_specs, out_specs, out_shape, scratch, flops, moved, aliases=None):
    return pl.pallas_call(
        kernel,
        out_shape=out_shape,
        grid_spec=pltpu.PrefetchScalarGridSpec(
            num_scalar_prefetch=1,
            grid=grid,
            in_specs=in_specs,
            out_specs=out_specs,
            scratch_shapes=scratch,
        ),
        input_output_aliases=aliases or {},
        compiler_params=params(name),
        cost_estimate=cost(flops, moved),
        name=name,
    )


def fixed(i, s):
    return (0, 0)


OWN, OTHER, SAME = 0, 1, 2


def column(chunk, side):
    first, size = chunk
    if side == SAME:
        return lambda s: first // size
    return lambda s: first // size + (s[0] if side == OWN else 1 - s[0])


def dispatch_kernel(experts, capacity, where_ref, route_ref, prob_ref, grad_ref,
                    send_ref, slot_ref, pick_ref):
    top, tokens = route_ref.shape
    expert = lax.broadcasted_iota(jnp.int32, (experts, tokens), 0)
    chosen = jnp.zeros((experts, tokens), F32)
    prob = jnp.zeros((experts, tokens), F32)
    for k in range(top):
        hit = route_ref[k : k + 1, :] == expert
        chosen = jnp.where(hit, 1.0, chosen)
        prob = jnp.where(hit, prob_ref[k : k + 1, :].astype(F32), prob)
    row = lax.broadcasted_iota(jnp.int32, (tokens, tokens), 0)
    col = lax.broadcasted_iota(jnp.int32, (tokens, tokens), 1)
    earlier = (row < col).astype(BF16)
    before = jnp.dot(chosen.astype(BF16), earlier, preferred_element_type=F32)
    slot = jnp.where(chosen > 0.5, before, -1.0)
    slot_ref[...] = slot
    place = lax.broadcasted_iota(jnp.int32, (capacity, tokens), 0).astype(F32)
    for e in range(experts):
        pick_ref[pl.ds(e * capacity, capacity), :] = jnp.where(
            slot[e : e + 1, :] == place, prob[e : e + 1, :], 0.0
        ).astype(BF16)
    send_ref[...] = jnp.dot(
        pick_ref[...], grad_ref[...], preferred_element_type=F32
    ).astype(BF16)


def dispatch(where, route, prob, grad, experts, capacity):
    tokens, width = grad.shape
    at = column(SHARED[0], OWN)
    part = SHARED[0][1]
    total = experts * capacity
    return call(
        functools.partial(dispatch_kernel, experts, capacity),
        "dispatch",
        (1,),
        [
            pl.BlockSpec(route.shape, fixed),
            pl.BlockSpec(prob.shape, fixed),
            pl.BlockSpec((tokens, part), lambda i, s: (0, at(s))),
        ],
        [
            pl.BlockSpec((total, part), fixed),
            pl.BlockSpec((experts, tokens), fixed),
            pl.BlockSpec((total, tokens), fixed),
        ],
        [
            jax.ShapeDtypeStruct((total, part), BF16),
            jax.ShapeDtypeStruct((experts, tokens), F32),
            jax.ShapeDtypeStruct((total, tokens), BF16),
        ],
        [],
        2 * total * tokens * part,
        2 * total * part,
    )(where, route, prob, grad)


def more_kernel(where_ref, pick_ref, grad_ref, send_ref):
    send_ref[...] = jnp.dot(
        pick_ref[...], grad_ref[...], preferred_element_type=F32
    ).astype(BF16)


def dispatch_more(where, pick, grad, chunk, side):
    total, tokens = pick.shape
    part = chunk[1]
    at = column(chunk, side)
    return call(
        more_kernel,
        "dispatch_more",
        (2,),
        [
            pl.BlockSpec((total // 2, tokens), lambda i, s: (i, 0)),
            pl.BlockSpec((tokens, part), lambda i, s: (0, at(s))),
        ],
        pl.BlockSpec((total // 2, part), lambda i, s: (i, 0)),
        jax.ShapeDtypeStruct((total, part), BF16),
        [],
        4,
        4,
    )(where, pick, grad)


def over_blocks(shape, body):
    def step(i, _):
        at = pl.ds(pl.multiple_of(i * SUB, SUB), SUB)
        for c in range(0, shape[1], COLS):
            body(at, pl.ds(c, COLS))
        return 0

    lax.fori_loop(0, shape[0] // SUB, step, 0)


def act_kernel(where_ref, gate_ref, up_ref, other_ref, mine_ref):
    def fill(out_ref):
        def body(at, cols):
            gate = gate_ref[at, cols].astype(F32)
            sig = 0.5 * jnp.tanh(0.5 * gate) + 0.5
            out_ref[at, cols] = (gate * sig * up_ref[at, cols].astype(F32)).astype(BF16)

        over_blocks(gate_ref.shape, body)

    @pl.when(pl.program_id(0) == 0)
    def _():
        fill(other_ref)

    @pl.when(pl.program_id(0) == 1)
    def _():
        fill(mine_ref)


def activation(where, gate, up):
    ff, slots = gate.shape
    tiles = ff // 2 // TILE_FF
    side = lambda h, s: h * s[2] + (1 - h) * (1 - s[2])
    spec = pl.BlockSpec((TILE_FF, slots), lambda h, n, s: (side(h, s) * tiles + n, 0))
    out = jax.ShapeDtypeStruct((ff // 2, slots), BF16)
    return pl.pallas_call(
        act_kernel,
        out_shape=[out, out],
        grid_spec=pltpu.PrefetchScalarGridSpec(
            num_scalar_prefetch=1,
            grid=(2, tiles),
            in_specs=[spec, spec],
            out_specs=[
                pl.BlockSpec((TILE_FF, slots), lambda h, n, s: (jnp.where(h == 0, n, tiles - 1), 0)),
                pl.BlockSpec((TILE_FF, slots), lambda h, n, s: (jnp.where(h == 0, 0, n), 0)),
            ],
        ),
        compiler_params=pltpu.CompilerParams(
            dimension_semantics=("arbitrary", "arbitrary"), vmem_limit_bytes=VMEM_MB["activation"] << 20
        ),
        cost_estimate=cost(4, 4),
        name="activation",
    )(where, gate, up)


def piece_specs(pieces, slots):
    specs = []
    for _, chunk, side in pieces:
        at = column(chunk, side)
        specs.append(pl.BlockSpec((slots, chunk[1]), fixed))
        specs.append(pl.BlockSpec((TILE_FF, chunk[1]), lambda n, s, at=at: (n, at(s))))
    return specs


def piece_dots(refs, count):
    total = None
    for p in range(count):
        term = lax.dot_general(
            refs[2 * p + 1][...], refs[2 * p][...], NT, preferred_element_type=F32
        )
        total = term if total is None else total + term
    return total


def raw_kernel(count, more, where_ref, *refs):
    total = piece_dots(refs, count)
    if more:
        total += refs[2 * count][...]
    refs[-1][...] = total


def raw_part(where, w, pieces, before=None):
    slots = pieces[0][0].shape[0]
    ff, width = w.shape
    depth = sum(chunk[1] for _, chunk, _ in pieces)
    tile = pl.BlockSpec((TILE_FF, slots), lambda n, s: (n, 0))
    args = [x for rows, _, _ in pieces for x in (rows, w)]
    more = before is not None
    return call(
        functools.partial(raw_kernel, len(pieces), more),
        "raw",
        (ff // TILE_FF,),
        piece_specs(pieces, slots) + ([tile] if more else []),
        tile,
        jax.ShapeDtypeStruct((ff, slots), F32),
        [],
        2 * slots * ff * depth,
        2 * (ff + slots) * depth + 8 * ff * slots,
    )(where, *args, *([before] if more else []))


def finish_kernel(count, where_ref, gate_ref, up_ref, before_ref, *refs):
    gg_ref, gu_ref, part_ref, acc = refs[2 * count :]
    tile, slots = gate_ref.shape

    @pl.when(pl.program_id(0) == 0)
    def _():
        acc[...] = jnp.zeros_like(acc)

    for c in range(0, slots, COLS):
        cols = pl.ds(c, COLS)
        raw = before_ref[:, cols]
        for p in range(count):
            raw += lax.dot_general(
                refs[2 * p + 1][...], refs[2 * p][cols, :], NT, preferred_element_type=F32
            )
        total = jnp.zeros((8, COLS), F32)
        for r in range(0, tile, SUB):
            at = pl.ds(r, SUB)
            gate = gate_ref[at, cols].astype(F32)
            upper = up_ref[at, cols].astype(F32)
            value = raw[r : r + SUB]
            sig = 0.5 * jnp.tanh(0.5 * gate) + 0.5
            gs = gate * sig
            gu_ref[at, cols] = (value * gs).astype(BF16)
            gg_ref[at, cols] = (value * upper * (sig + gs * (1.0 - sig))).astype(BF16)
            term = value * (gs * upper)
            total += term[:8] + term[8:]
        acc[:, cols] += total

    @pl.when(pl.program_id(0) == pl.num_programs(0) - 1)
    def _():
        total = jnp.sum(acc[...], axis=0, keepdims=True)
        groups, capacity = part_ref.shape
        for g in range(groups):
            part_ref[g : g + 1, :] = total[:, g * capacity : (g + 1) * capacity]


def finish(where, gate, up, before, w, pieces, groups):
    ff, slots = gate.shape
    depth = sum(chunk[1] for _, chunk, _ in pieces)
    tile = pl.BlockSpec((TILE_FF, slots), lambda n, s: (n, 0))
    args = [x for rows, _, _ in pieces for x in (rows, w)]
    return call(
        functools.partial(finish_kernel, len(pieces)),
        "finish",
        (ff // TILE_FF,),
        [tile, tile, tile] + piece_specs(pieces, slots),
        [tile, tile, pl.BlockSpec((groups, slots // groups), fixed)],
        [
            jax.ShapeDtypeStruct((ff, slots), BF16),
            jax.ShapeDtypeStruct((ff, slots), BF16),
            jax.ShapeDtypeStruct((groups, slots // groups), F32),
        ],
        [pltpu.VMEM((8, slots), F32)],
        2 * slots * ff * depth,
        2 * (ff + slots) * depth + 12 * ff * slots,
    )(where, gate, up, before, *args)


def down_kernel(counts, where_ref, here_ref, there_ref, *refs):
    at = 0
    for p, count in enumerate(counts):

        @pl.when((pl.program_id(0) >= at) & (pl.program_id(0) < at + count))
        def _(p=p):
            total = jnp.dot(here_ref[...], refs[2 * p][...], preferred_element_type=F32)
            total += jnp.dot(there_ref[...], refs[2 * p + 1][...], preferred_element_type=F32)
            refs[-1][...] = total.astype(BF16)

        at += count


def down(where, acts, pieces, width, into=None):
    half_ff, slots = acts[0].shape
    counts = [chunk[1] // TILE_D for _, _, chunk, _ in pieces]
    tiles = sum(counts)
    in_specs = [pl.BlockSpec((half_ff, slots), fixed)] * 2
    args = [where, *acts]
    starts = []
    for p, (here, there, _, _) in enumerate(pieces):
        start = sum(counts[:p])
        starts.append(start)
        place = lambda i, s, a=start, n=counts[p]: (0, jnp.clip(i - a, 0, n - 1))
        in_specs += [pl.BlockSpec((slots, TILE_D), place)] * 2
        args += [here, there]

    def place_out(i, s):
        at = 0
        for (_, _, chunk, side), start, count in zip(pieces, starts, counts):
            first = column(chunk, side)(s) * count
            at = jnp.where((i >= start) & (i < start + count), first + i - start, at)
        return (0, at)

    aliases = {}
    if into is not None:
        in_specs.append(pl.BlockSpec(memory_space=pl.ANY))
        aliases = {len(args): 0}
        args.append(into)
    return call(
        functools.partial(down_kernel, counts),
        "down",
        (tiles,),
        in_specs,
        pl.BlockSpec((half_ff, TILE_D), place_out),
        jax.ShapeDtypeStruct((half_ff, width), BF16),
        [],
        4 * half_ff * TILE_D * slots * tiles,
        2 * (half_ff * TILE_D + 2 * slots * TILE_D) * tiles + 4 * slots * half_ff,
        aliases,
    )(*args)


def combine_kernel(experts, route_ref, prob_ref, slot_ref, *refs):
    out_ref = refs[-1]
    values = refs[0][...]
    for ref in refs[1:-1]:
        values += ref[...]
    capacity = values.shape[1]
    tokens = route_ref.shape[1]
    columns = values.T
    place = lax.broadcasted_iota(jnp.int32, (capacity, tokens), 0).astype(F32)
    route = route_ref[...]
    total = jnp.zeros(route.shape, F32)
    for e in range(experts):
        hit = slot_ref[e : e + 1, :] == place
        mine = jnp.sum(jnp.where(hit, columns[:, e : e + 1], 0.0), axis=0, keepdims=True)
        total = jnp.where(route == e, mine, total)
    out_ref[...] = total / prob_ref[...].astype(F32)


def combine(route, prob, slot, values):
    experts = values[0].shape[0]
    return pl.pallas_call(
        functools.partial(combine_kernel, experts),
        out_shape=jax.ShapeDtypeStruct(route.shape, F32),
        name="combine",
    )(route, prob, slot, *values)


def local(out_grad, route, gate_prob, w_down, gate_pre, up_pre):
    experts = lax.axis_size("expert")
    etp = lax.axis_size("etp")
    slots, ff = gate_pre.shape[1:]
    capacity = slots // experts
    width = out_grad.shape[1]
    where = jnp.stack(
        [lax.axis_index("etp") % 2, lax.axis_index("expert"), lax.axis_index("dp")]
    ).astype(jnp.int32)
    gate, up, w = gate_pre[0].T, up_pre[0].T, w_down[0]
    route, prob = route.T, gate_prob.T

    swap = [(2 * i, 2 * ((i - 1) % etp)) for i in range(etp)]
    swap += [(2 * i + 1, 2 * ((i + 1) % etp) + 1) for i in range(etp)]

    def fetch(send):
        x = send.reshape(experts, capacity, send.shape[1])
        x = lax.all_to_all(x, "expert", split_axis=0, concat_axis=0, tiled=True)
        return x.reshape(send.shape)

    def beside(x):
        return lax.ppermute(x, ("etp", "dp"), swap)

    def swap_dp(x):
        return lax.ppermute(x, "dp", [(0, 1), (1, 0)])

    c0, c1 = SHARED
    first, slot, pick = dispatch(where, route, prob, out_grad, experts, capacity)
    gate, up, pick = lax.optimization_barrier((gate, up, pick))
    own0 = fetch(first)
    send1 = dispatch_more(where, pick, out_grad, c1, OWN)
    send2 = dispatch_more(where, pick, out_grad, DIRECT, SAME)
    act_other, act_mine = activation(where, gate, up)
    own0, send1, send2, act_other, act_mine = lax.optimization_barrier(
        (own0, send1, send2, act_other, act_mine)
    )
    acts = (act_mine, swap_dp(act_other))
    own1 = fetch(send1)
    oth0 = beside(own0)
    total = down(where, acts, [(own0, swap_dp(own0), c0, OWN)], width)
    total = down(where, acts, [(oth0, swap_dp(oth0), c0, OTHER)], width, total)
    own1, send2, total = lax.optimization_barrier((own1, send2, total))
    direct = fetch(send2)
    oth1 = beside(own1)
    raw = raw_part(where, w, [(own0, c0, OWN), (own1, c1, OWN), (oth0, c0, OTHER)])
    pieces = [(own1, swap_dp(own1), c1, OWN)]
    total = down(where, acts, pieces, width, total)
    direct, oth1, raw, total = lax.optimization_barrier((direct, oth1, raw, total))
    late = [(oth1, c1, OTHER), (direct, DIRECT, SAME)]
    grad_gate, grad_up, sums = finish(where, gate, up, raw, w, late, experts)
    back = lax.all_to_all(sums, "expert", split_axis=0, concat_axis=0, tiled=True)
    pieces = [(rows, swap_dp(rows), chunk, side) for rows, chunk, side in late]
    total = down(where, acts, pieces[:1], width, total)
    back, total = lax.optimization_barrier((back, total))
    others = [
        lax.ppermute(back, "etp", [(i, (i + k) % etp) for i in range(etp)]) for k in range(1, etp)
    ]
    total = down(where, acts, pieces[1:], width, total)
    others, total = lax.optimization_barrier((others, total))
    grad_prob = combine(route, prob, slot, [back, *others])
    return grad_gate.T[None], grad_up.T[None], total[None], grad_prob.T


def solution(mesh):
    in_specs = (
        P(("expert", "dp"), None),
        P(("expert", "dp"), None),
        P(("expert", "dp"), None),
        P("expert", "etp", None),
        P("expert", "dp", "etp"),
        P("expert", "dp", "etp"),
    )
    out_specs = (
        P("expert", "dp", "etp"),
        P("expert", "dp", "etp"),
        P("expert", ("etp", "dp"), None),
        P(("expert", "dp"), None),
    )
    return jax.shard_map(local, mesh=mesh, in_specs=in_specs, out_specs=out_specs, check_vma=False)
```

```python
import functools

import jax
import jax.numpy as jnp
from jax import lax
from jax.experimental import pallas as pl
from jax.experimental.pallas import tpu as pltpu
from jax.sharding import PartitionSpec as P

BF16 = jnp.bfloat16
F32 = jnp.float32
LANES = 128
SHARED = ((0, 512), (1536, 768))
DIRECT = (1024, 512)
TILE_FF = 336
TILE_D = 256
SUB = 16
COLS = 256
VMEM_MB = {"dispatch": 16, "dispatch_more": 12, "activation": 16, "raw": 56, "finish": 56, "down": 20}
NT = (((1,), (1,)), ((), ()))


def params(name):
    return pltpu.CompilerParams(
        dimension_semantics=("arbitrary",), vmem_limit_bytes=VMEM_MB[name] << 20
    )


def cost(flops, moved):
    flops, moved = flops // 4, moved // 4
    return pl.CostEstimate(flops=flops, bytes_accessed=moved, transcendentals=0)


def call(kernel, name, grid, in_specs, out_specs, out_shape, scratch, flops, moved, aliases=None):
    return pl.pallas_call(
        kernel,
        out_shape=out_shape,
        grid_spec=pltpu.PrefetchScalarGridSpec(
            num_scalar_prefetch=1,
            grid=grid,
            in_specs=in_specs,
            out_specs=out_specs,
            scratch_shapes=scratch,
        ),
        input_output_aliases=aliases or {},
        compiler_params=params(name),
        cost_estimate=cost(flops, moved),
        name=name,
    )


def fixed(i, s):
    return (0, 0)


OWN, OTHER, SAME = 0, 1, 2


def column(chunk, side):
    first, size = chunk
    if side == SAME:
        return lambda s: first // size
    return lambda s: first // size + (s[0] if side == OWN else 1 - s[0])


def dispatch_kernel(experts, capacity, where_ref, route_ref, prob_ref, grad_ref,
                    send_ref, slot_ref, pick_ref):
    top, tokens = route_ref.shape
    expert = lax.broadcasted_iota(jnp.int32, (experts, tokens), 0)
    chosen = jnp.zeros((experts, tokens), F32)
    prob = jnp.zeros((experts, tokens), F32)
    for k in range(top):
        hit = route_ref[k : k + 1, :] == expert
        chosen = jnp.where(hit, 1.0, chosen)
        prob = jnp.where(hit, prob_ref[k : k + 1, :].astype(F32), prob)
    row = lax.broadcasted_iota(jnp.int32, (tokens, tokens), 0)
    col = lax.broadcasted_iota(jnp.int32, (tokens, tokens), 1)
    earlier = (row < col).astype(BF16)
    before = jnp.dot(chosen.astype(BF16), earlier, preferred_element_type=F32)
    slot = jnp.where(chosen > 0.5, before, -1.0)
    slot_ref[...] = slot
    place = lax.broadcasted_iota(jnp.int32, (capacity, tokens), 0).astype(F32)
    for e in range(experts):
        pick_ref[pl.ds(e * capacity, capacity), :] = jnp.where(
            slot[e : e + 1, :] == place, prob[e : e + 1, :], 0.0
        ).astype(BF16)
    send_ref[...] = jnp.dot(
        pick_ref[...], grad_ref[...], preferred_element_type=F32
    ).astype(BF16)


def dispatch(where, route, prob, grad, experts, capacity):
    tokens, width = grad.shape
    at = column(SHARED[0], OWN)
    part = SHARED[0][1]
    total = experts * capacity
    return call(
        functools.partial(dispatch_kernel, experts, capacity),
        "dispatch",
        (1,),
        [
            pl.BlockSpec(route.shape, fixed),
            pl.BlockSpec(prob.shape, fixed),
            pl.BlockSpec((tokens, part), lambda i, s: (0, at(s))),
        ],
        [
            pl.BlockSpec((total, part), fixed),
            pl.BlockSpec((experts, tokens), fixed),
            pl.BlockSpec((total, tokens), fixed),
        ],
        [
            jax.ShapeDtypeStruct((total, part), BF16),
            jax.ShapeDtypeStruct((experts, tokens), F32),
            jax.ShapeDtypeStruct((total, tokens), BF16),
        ],
        [],
        2 * total * tokens * part,
        2 * total * part,
    )(where, route, prob, grad)


def more_kernel(where_ref, pick_ref, grad_ref, send_ref):
    send_ref[...] = jnp.dot(
        pick_ref[...], grad_ref[...], preferred_element_type=F32
    ).astype(BF16)


def dispatch_more(where, pick, grad, chunk, side):
    total, tokens = pick.shape
    part = chunk[1]
    at = column(chunk, side)
    return call(
        more_kernel,
        "dispatch_more",
        (2,),
        [
            pl.BlockSpec((total // 2, tokens), lambda i, s: (i, 0)),
            pl.BlockSpec((tokens, part), lambda i, s: (0, at(s))),
        ],
        pl.BlockSpec((total // 2, part), lambda i, s: (i, 0)),
        jax.ShapeDtypeStruct((total, part), BF16),
        [],
        4,
        4,
    )(where, pick, grad)


def over_blocks(shape, body):
    def step(i, _):
        at = pl.ds(pl.multiple_of(i * SUB, SUB), SUB)
        for c in range(0, shape[1], COLS):
            body(at, pl.ds(c, COLS))
        return 0

    lax.fori_loop(0, shape[0] // SUB, step, 0)


def act_kernel(where_ref, gate_ref, up_ref, other_ref, mine_ref):
    def fill(out_ref):
        def body(at, cols):
            gate = gate_ref[at, cols].astype(F32)
            sig = 0.5 * jnp.tanh(0.5 * gate) + 0.5
            out_ref[at, cols] = (gate * sig * up_ref[at, cols].astype(F32)).astype(BF16)

        over_blocks(gate_ref.shape, body)

    @pl.when(pl.program_id(0) == 0)
    def _():
        fill(other_ref)

    @pl.when(pl.program_id(0) == 1)
    def _():
        fill(mine_ref)


def activation(where, gate, up):
    ff, slots = gate.shape
    tiles = ff // 2 // TILE_FF
    side = lambda h, s: h * s[2] + (1 - h) * (1 - s[2])
    spec = pl.BlockSpec((TILE_FF, slots), lambda h, n, s: (side(h, s) * tiles + n, 0))
    out = jax.ShapeDtypeStruct((ff // 2, slots), BF16)
    return pl.pallas_call(
        act_kernel,
        out_shape=[out, out],
        grid_spec=pltpu.PrefetchScalarGridSpec(
            num_scalar_prefetch=1,
            grid=(2, tiles),
            in_specs=[spec, spec],
            out_specs=[
                pl.BlockSpec((TILE_FF, slots), lambda h, n, s: (jnp.where(h == 0, n, tiles - 1), 0)),
                pl.BlockSpec((TILE_FF, slots), lambda h, n, s: (jnp.where(h == 0, 0, n), 0)),
            ],
        ),
        compiler_params=pltpu.CompilerParams(
            dimension_semantics=("arbitrary", "arbitrary"), vmem_limit_bytes=VMEM_MB["activation"] << 20
        ),
        cost_estimate=cost(4, 4),
        name="activation",
    )(where, gate, up)


def piece_specs(pieces, slots):
    specs = []
    for _, chunk, side in pieces:
        at = column(chunk, side)
        specs.append(pl.BlockSpec((slots, chunk[1]), fixed))
        specs.append(pl.BlockSpec((TILE_FF, chunk[1]), lambda n, s, at=at: (n, at(s))))
    return specs


def piece_dots(refs, count):
    total = None
    for p in range(count):
        term = lax.dot_general(
            refs[2 * p + 1][...], refs[2 * p][...], NT, preferred_element_type=F32
        )
        total = term if total is None else total + term
    return total


def raw_kernel(count, more, where_ref, *refs):
    total = piece_dots(refs, count)
    if more:
        total += refs[2 * count][...]
    refs[-1][...] = total


def raw_part(where, w, pieces, before=None):
    slots = pieces[0][0].shape[0]
    ff, width = w.shape
    depth = sum(chunk[1] for _, chunk, _ in pieces)
    tile = pl.BlockSpec((TILE_FF, slots), lambda n, s: (n, 0))
    args = [x for rows, _, _ in pieces for x in (rows, w)]
    more = before is not None
    return call(
        functools.partial(raw_kernel, len(pieces), more),
        "raw",
        (ff // TILE_FF,),
        piece_specs(pieces, slots) + ([tile] if more else []),
        tile,
        jax.ShapeDtypeStruct((ff, slots), F32),
        [],
        2 * slots * ff * depth,
        2 * (ff + slots) * depth + 8 * ff * slots,
    )(where, *args, *([before] if more else []))


def finish_kernel(count, where_ref, gate_ref, up_ref, before_ref, *refs):
    gg_ref, gu_ref, part_ref, acc = refs[2 * count :]
    tile, slots = gate_ref.shape

    @pl.when(pl.program_id(0) == 0)
    def _():
        acc[...] = jnp.zeros_like(acc)

    for c in range(0, slots, COLS):
        cols = pl.ds(c, COLS)
        raw = before_ref[:, cols]
        for p in range(count):
            raw += lax.dot_general(
                refs[2 * p + 1][...], refs[2 * p][cols, :], NT, preferred_element_type=F32
            )
        total = jnp.zeros((8, COLS), F32)
        for r in range(0, tile, SUB):
            at = pl.ds(r, SUB)
            gate = gate_ref[at, cols].astype(F32)
            upper = up_ref[at, cols].astype(F32)
            value = raw[r : r + SUB]
            sig = 0.5 * jnp.tanh(0.5 * gate) + 0.5
            gs = gate * sig
            gu_ref[at, cols] = (value * gs).astype(BF16)
            gg_ref[at, cols] = (value * upper * (sig + gs * (1.0 - sig))).astype(BF16)
            term = value * (gs * upper)
            total += term[:8] + term[8:]
        acc[:, cols] += total

    @pl.when(pl.program_id(0) == pl.num_programs(0) - 1)
    def _():
        total = jnp.sum(acc[...], axis=0, keepdims=True)
        copies, groups, capacity = part_ref.shape
        for g in range(groups):
            sums = total[:, g * capacity : (g + 1) * capacity]
            for x in range(copies):
                part_ref[x, g : g + 1, :] = sums


def finish(where, gate, up, before, w, pieces, groups, copies):
    ff, slots = gate.shape
    depth = sum(chunk[1] for _, chunk, _ in pieces)
    tile = pl.BlockSpec((TILE_FF, slots), lambda n, s: (n, 0))
    args = [x for rows, _, _ in pieces for x in (rows, w)]
    return call(
        functools.partial(finish_kernel, len(pieces)),
        "finish",
        (ff // TILE_FF,),
        [tile, tile, tile] + piece_specs(pieces, slots),
        [tile, tile, pl.BlockSpec((copies, groups, slots // groups), lambda n, s: (0, 0, 0))],
        [
            jax.ShapeDtypeStruct((ff, slots), BF16),
            jax.ShapeDtypeStruct((ff, slots), BF16),
            jax.ShapeDtypeStruct((copies, groups, slots // groups), F32),
        ],
        [pltpu.VMEM((8, slots), F32)],
        2 * slots * ff * depth,
        2 * (ff + slots) * depth + 12 * ff * slots,
    )(where, gate, up, before, *args)


def down_kernel(counts, where_ref, here_ref, there_ref, *refs):
    at = 0
    for p, count in enumerate(counts):

        @pl.when((pl.program_id(0) >= at) & (pl.program_id(0) < at + count))
        def _(p=p):
            total = jnp.dot(here_ref[...], refs[2 * p][...], preferred_element_type=F32)
            total += jnp.dot(there_ref[...], refs[2 * p + 1][...], preferred_element_type=F32)
            refs[-1][...] = total.astype(BF16)

        at += count


def down(where, acts, pieces, width, into=None):
    half_ff, slots = acts[0].shape
    counts = [chunk[1] // TILE_D for _, _, chunk, _ in pieces]
    tiles = sum(counts)
    in_specs = [pl.BlockSpec((half_ff, slots), fixed)] * 2
    args = [where, *acts]
    starts = []
    for p, (here, there, _, _) in enumerate(pieces):
        start = sum(counts[:p])
        starts.append(start)
        place = lambda i, s, a=start, n=counts[p]: (0, jnp.clip(i - a, 0, n - 1))
        in_specs += [pl.BlockSpec((slots, TILE_D), place)] * 2
        args += [here, there]

    def place_out(i, s):
        at = 0
        for (_, _, chunk, side), start, count in zip(pieces, starts, counts):
            first = column(chunk, side)(s) * count
            at = jnp.where((i >= start) & (i < start + count), first + i - start, at)
        return (0, at)

    aliases = {}
    if into is not None:
        in_specs.append(pl.BlockSpec(memory_space=pl.ANY))
        aliases = {len(args): 0}
        args.append(into)
    return call(
        functools.partial(down_kernel, counts),
        "down",
        (tiles,),
        in_specs,
        pl.BlockSpec((half_ff, TILE_D), place_out),
        jax.ShapeDtypeStruct((half_ff, width), BF16),
        [],
        4 * half_ff * TILE_D * slots * tiles,
        2 * (half_ff * TILE_D + 2 * slots * TILE_D) * tiles + 4 * slots * half_ff,
        aliases,
    )(*args)


def combine_kernel(experts, route_ref, prob_ref, slot_ref, values_ref, out_ref):
    values = values_ref[0]
    for x in range(1, values_ref.shape[0]):
        values += values_ref[x]
    capacity = values.shape[1]
    tokens = route_ref.shape[1]
    columns = values.T
    place = lax.broadcasted_iota(jnp.int32, (capacity, tokens), 0).astype(F32)
    route = route_ref[...]
    total = jnp.zeros(route.shape, F32)
    for e in range(experts):
        hit = slot_ref[e : e + 1, :] == place
        mine = jnp.sum(jnp.where(hit, columns[:, e : e + 1], 0.0), axis=0, keepdims=True)
        total = jnp.where(route == e, mine, total)
    out_ref[...] = total / prob_ref[...].astype(F32)


def combine(route, prob, slot, values):
    experts = values.shape[1]
    return pl.pallas_call(
        functools.partial(combine_kernel, experts),
        out_shape=jax.ShapeDtypeStruct(route.shape, F32),
        name="combine",
    )(route, prob, slot, values)


def local(out_grad, route, gate_prob, w_down, gate_pre, up_pre):
    experts = lax.axis_size("expert")
    etp = lax.axis_size("etp")
    slots, ff = gate_pre.shape[1:]
    capacity = slots // experts
    width = out_grad.shape[1]
    parity = lax.bitwise_and(lax.axis_index("etp"), 1).reshape(1)
    where = jnp.concatenate([parity, parity, lax.axis_index("dp").reshape(1)])
    gate, up, w = gate_pre[0].T, up_pre[0].T, w_down[0]
    route, prob = route.T, gate_prob.T

    swap = [(2 * i, 2 * ((i - 1) % etp)) for i in range(etp)]
    swap += [(2 * i + 1, 2 * ((i + 1) % etp) + 1) for i in range(etp)]

    def fetch(send):
        x = send.reshape(experts, capacity, send.shape[1])
        x = lax.all_to_all(x, "expert", split_axis=0, concat_axis=0, tiled=True)
        return x.reshape(send.shape)

    def beside(x):
        return lax.ppermute(x, ("etp", "dp"), swap)

    def swap_dp(x):
        return lax.ppermute(x, "dp", [(0, 1), (1, 0)])

    c0, c1 = SHARED
    first, slot, pick = dispatch(parity, route, prob, out_grad, experts, capacity)
    gate, up, pick = lax.optimization_barrier((gate, up, pick))
    own0 = fetch(first)
    send1 = dispatch_more(parity, pick, out_grad, c1, OWN)
    send2 = dispatch_more(parity, pick, out_grad, DIRECT, SAME)
    act_other, act_mine = activation(where, gate, up)
    own0, send1, send2, act_other, act_mine = lax.optimization_barrier(
        (own0, send1, send2, act_other, act_mine)
    )
    acts = (act_mine, swap_dp(act_other))
    own1 = fetch(send1)
    oth0 = beside(own0)
    total = down(where, acts, [(own0, swap_dp(own0), c0, OWN)], width)
    total = down(where, acts, [(oth0, swap_dp(oth0), c0, OTHER)], width, total)
    own1, send2, total = lax.optimization_barrier((own1, send2, total))
    direct = fetch(send2)
    oth1 = beside(own1)
    raw = raw_part(where, w, [(own0, c0, OWN), (own1, c1, OWN), (oth0, c0, OTHER)])
    pieces = [(own1, swap_dp(own1), c1, OWN)]
    total = down(where, acts, pieces, width, total)
    direct, oth1, raw, total = lax.optimization_barrier((direct, oth1, raw, total))
    late = [(oth1, c1, OTHER), (direct, DIRECT, SAME)]
    grad_gate, grad_up, sums = finish(where, gate, up, raw, w, late, experts, etp)
    sums = sums.reshape(etp * experts, capacity)
    back = lax.all_to_all(sums, ("etp", "expert"), split_axis=0, concat_axis=0, tiled=True)
    pieces = [(rows, swap_dp(rows), chunk, side) for rows, chunk, side in late]
    total = down(where, acts, pieces, width, total)
    back, total = lax.optimization_barrier((back, total))
    grad_prob = combine(route, prob, slot, back.reshape(etp, experts, capacity))
    return grad_gate.T[None], grad_up.T[None], total[None], grad_prob.T


def solution(mesh):
    in_specs = (
        P(("expert", "dp"), None),
        P(("expert", "dp"), None),
        P(("expert", "dp"), None),
        P("expert", "etp", None),
        P("expert", "dp", "etp"),
        P("expert", "dp", "etp"),
    )
    out_specs = (
        P("expert", "dp", "etp"),
        P("expert", "dp", "etp"),
        P("expert", ("etp", "dp"), None),
        P(("expert", "dp"), None),
    )
    return jax.shard_map(local, mesh=mesh, in_specs=in_specs, out_specs=out_specs, check_vma=False)
```

```python
import functools

import jax
import jax.numpy as jnp
from jax import lax
from jax.experimental import pallas as pl
from jax.experimental.pallas import tpu as pltpu
from jax.sharding import PartitionSpec as P

BF16 = jnp.bfloat16
F32 = jnp.float32
LANES = 128
SHARED = ((0, 512), (1536, 768))
DIRECT = (1024, 512)
TILE_FF = 336
TILE_D = 256
STEPS = 4
SUB = 16
COLS = 256
VMEM_MB = {"dispatch": 16, "dispatch_more": 12, "activation": 16, "raw": 56, "finish": 56, "down": 20}
NT = (((1,), (1,)), ((), ()))


def params(name):
    return pltpu.CompilerParams(
        dimension_semantics=("arbitrary",), vmem_limit_bytes=VMEM_MB[name] << 20
    )


def cost(flops, moved):
    flops, moved = flops // 4, moved // 4
    return pl.CostEstimate(flops=flops, bytes_accessed=moved, transcendentals=0)


def call(kernel, name, grid, in_specs, out_specs, out_shape, scratch, flops, moved, aliases=None):
    return pl.pallas_call(
        kernel,
        out_shape=out_shape,
        grid_spec=pltpu.PrefetchScalarGridSpec(
            num_scalar_prefetch=1,
            grid=grid,
            in_specs=in_specs,
            out_specs=out_specs,
            scratch_shapes=scratch,
        ),
        input_output_aliases=aliases or {},
        compiler_params=params(name),
        cost_estimate=cost(flops, moved),
        name=name,
    )


def fixed(i, s):
    return (0, 0)


OWN, OTHER, SAME = 0, 1, 2


def column(chunk, side):
    first, size = chunk
    if side == SAME:
        return lambda s: first // size
    return lambda s: first // size + (s[0] if side == OWN else 1 - s[0])


def dispatch_kernel(experts, capacity, where_ref, route_ref, prob_ref, grad_ref,
                    send_ref, slot_ref, pick_ref, weight):
    top, tokens = route_ref.shape
    step = pl.program_id(0)
    group = experts // pl.num_programs(0)

    @pl.when(step == 0)
    def _():
        expert = lax.broadcasted_iota(jnp.int32, (experts, tokens), 0)
        chosen = jnp.zeros((experts, tokens), F32)
        prob = jnp.zeros((experts, tokens), F32)
        for k in range(top):
            hit = route_ref[k : k + 1, :] == expert
            chosen = jnp.where(hit, 1.0, chosen)
            prob = jnp.where(hit, prob_ref[k : k + 1, :].astype(F32), prob)
        row = lax.broadcasted_iota(jnp.int32, (tokens, tokens), 0)
        col = lax.broadcasted_iota(jnp.int32, (tokens, tokens), 1)
        earlier = (row < col).astype(BF16)
        before = jnp.dot(chosen.astype(BF16), earlier, preferred_element_type=F32)
        slot = jnp.where(chosen > 0.5, before, -1.0)
        slot_ref[...] = slot
        weight[...] = prob

    place = lax.broadcasted_iota(jnp.int32, (capacity, tokens), 0).astype(F32)
    for e in range(group):
        one = pl.ds(step * group + e, 1)
        pick_ref[pl.ds(e * capacity, capacity), :] = jnp.where(
            slot_ref[one, :] == place, weight[one, :], 0.0
        ).astype(BF16)
    send_ref[...] = jnp.dot(
        pick_ref[...], grad_ref[...], preferred_element_type=F32
    ).astype(BF16)


def dispatch(where, route, prob, grad, experts, capacity):
    tokens, width = grad.shape
    at = column(SHARED[0], OWN)
    part = SHARED[0][1]
    total = experts * capacity
    return call(
        functools.partial(dispatch_kernel, experts, capacity),
        "dispatch",
        (STEPS,),
        [
            pl.BlockSpec(route.shape, fixed),
            pl.BlockSpec(prob.shape, fixed),
            pl.BlockSpec((tokens, part), lambda i, s: (0, at(s))),
        ],
        [
            pl.BlockSpec((total // STEPS, part), lambda i, s: (i, 0)),
            pl.BlockSpec((experts, tokens), fixed),
            pl.BlockSpec((total // STEPS, tokens), lambda i, s: (i, 0)),
        ],
        [
            jax.ShapeDtypeStruct((total, part), BF16),
            jax.ShapeDtypeStruct((experts, tokens), F32),
            jax.ShapeDtypeStruct((total, tokens), BF16),
        ],
        [pltpu.VMEM((experts, tokens), F32)],
        2 * total * tokens * part,
        2 * total * part,
    )(where, route, prob, grad)


def more_kernel(where_ref, pick_ref, grad_ref, send_ref):
    send_ref[...] = jnp.dot(
        pick_ref[...], grad_ref[...], preferred_element_type=F32
    ).astype(BF16)


def dispatch_more(where, pick, grad, chunk, side):
    total, tokens = pick.shape
    part = chunk[1]
    at = column(chunk, side)
    return call(
        more_kernel,
        "dispatch_more",
        (2,),
        [
            pl.BlockSpec((total // 2, tokens), lambda i, s: (i, 0)),
            pl.BlockSpec((tokens, part), lambda i, s: (0, at(s))),
        ],
        pl.BlockSpec((total // 2, part), lambda i, s: (i, 0)),
        jax.ShapeDtypeStruct((total, part), BF16),
        [],
        4,
        4,
    )(where, pick, grad)


def over_blocks(shape, body):
    def step(i, _):
        at = pl.ds(pl.multiple_of(i * SUB, SUB), SUB)
        for c in range(0, shape[1], COLS):
            body(at, pl.ds(c, COLS))
        return 0

    lax.fori_loop(0, shape[0] // SUB, step, 0)


def act_kernel(where_ref, gate_ref, up_ref, other_ref, mine_ref):
    def fill(out_ref):
        def body(at, cols):
            gate = gate_ref[at, cols].astype(F32)
            sig = 0.5 * jnp.tanh(0.5 * gate) + 0.5
            out_ref[at, cols] = (gate * sig * up_ref[at, cols].astype(F32)).astype(BF16)

        over_blocks(gate_ref.shape, body)

    @pl.when(pl.program_id(0) == 0)
    def _():
        fill(other_ref)

    @pl.when(pl.program_id(0) == 1)
    def _():
        fill(mine_ref)


def activation(where, gate, up):
    ff, slots = gate.shape
    tiles = ff // 2 // TILE_FF
    side = lambda h, s: h * s[2] + (1 - h) * (1 - s[2])
    spec = pl.BlockSpec((TILE_FF, slots), lambda h, n, s: (side(h, s) * tiles + n, 0))
    out = jax.ShapeDtypeStruct((ff // 2, slots), BF16)
    return pl.pallas_call(
        act_kernel,
        out_shape=[out, out],
        grid_spec=pltpu.PrefetchScalarGridSpec(
            num_scalar_prefetch=1,
            grid=(2, tiles),
            in_specs=[spec, spec],
            out_specs=[
                pl.BlockSpec((TILE_FF, slots), lambda h, n, s: (jnp.where(h == 0, n, tiles - 1), 0)),
                pl.BlockSpec((TILE_FF, slots), lambda h, n, s: (jnp.where(h == 0, 0, n), 0)),
            ],
        ),
        compiler_params=pltpu.CompilerParams(
            dimension_semantics=("arbitrary", "arbitrary"), vmem_limit_bytes=VMEM_MB["activation"] << 20
        ),
        cost_estimate=cost(4, 4),
        name="activation",
    )(where, gate, up)


def piece_specs(pieces, slots):
    specs = []
    for _, chunk, side in pieces:
        at = column(chunk, side)
        specs.append(pl.BlockSpec((slots, chunk[1]), fixed))
        specs.append(pl.BlockSpec((TILE_FF, chunk[1]), lambda n, s, at=at: (n, at(s))))
    return specs


def piece_dots(refs, count):
    total = None
    for p in range(count):
        term = lax.dot_general(
            refs[2 * p + 1][...], refs[2 * p][...], NT, preferred_element_type=F32
        )
        total = term if total is None else total + term
    return total


def raw_kernel(count, more, where_ref, *refs):
    total = piece_dots(refs, count)
    if more:
        total += refs[2 * count][...]
    refs[-1][...] = total


def raw_part(where, w, pieces, before=None):
    slots = pieces[0][0].shape[0]
    ff, width = w.shape
    depth = sum(chunk[1] for _, chunk, _ in pieces)
    tile = pl.BlockSpec((TILE_FF, slots), lambda n, s: (n, 0))
    args = [x for rows, _, _ in pieces for x in (rows, w)]
    more = before is not None
    return call(
        functools.partial(raw_kernel, len(pieces), more),
        "raw",
        (ff // TILE_FF,),
        piece_specs(pieces, slots) + ([tile] if more else []),
        tile,
        jax.ShapeDtypeStruct((ff, slots), F32),
        [],
        2 * slots * ff * depth,
        2 * (ff + slots) * depth + 8 * ff * slots,
    )(where, *args, *([before] if more else []))


def finish_kernel(count, where_ref, gate_ref, up_ref, before_ref, *refs):
    gg_ref, gu_ref, part_ref, acc = refs[2 * count :]
    tile, slots = gate_ref.shape

    @pl.when(pl.program_id(0) == 0)
    def _():
        acc[...] = jnp.zeros_like(acc)

    for c in range(0, slots, COLS):
        cols = pl.ds(c, COLS)
        raw = before_ref[:, cols]
        for p in range(count):
            raw += lax.dot_general(
                refs[2 * p + 1][...], refs[2 * p][cols, :], NT, preferred_element_type=F32
            )
        total = jnp.zeros((8, COLS), F32)
        for r in range(0, tile, SUB):
            at = pl.ds(r, SUB)
            gate = gate_ref[at, cols].astype(F32)
            upper = up_ref[at, cols].astype(F32)
            value = raw[r : r + SUB]
            sig = 0.5 * jnp.tanh(0.5 * gate) + 0.5
            gs = gate * sig
            gu_ref[at, cols] = (value * gs).astype(BF16)
            gg_ref[at, cols] = (value * upper * (sig + gs * (1.0 - sig))).astype(BF16)
            term = value * (gs * upper)
            total += term[:8] + term[8:]
        acc[:, cols] += total

    @pl.when(pl.program_id(0) == pl.num_programs(0) - 1)
    def _():
        total = jnp.sum(acc[...], axis=0, keepdims=True)
        copies, groups, capacity = part_ref.shape
        for g in range(groups):
            sums = total[:, g * capacity : (g + 1) * capacity]
            for x in range(copies):
                part_ref[x, g : g + 1, :] = sums


def finish(where, gate, up, before, w, pieces, groups, copies):
    ff, slots = gate.shape
    depth = sum(chunk[1] for _, chunk, _ in pieces)
    tile = pl.BlockSpec((TILE_FF, slots), lambda n, s: (n, 0))
    args = [x for rows, _, _ in pieces for x in (rows, w)]
    return call(
        functools.partial(finish_kernel, len(pieces)),
        "finish",
        (ff // TILE_FF,),
        [tile, tile, tile] + piece_specs(pieces, slots),
        [tile, tile, pl.BlockSpec((copies, groups, slots // groups), lambda n, s: (0, 0, 0))],
        [
            jax.ShapeDtypeStruct((ff, slots), BF16),
            jax.ShapeDtypeStruct((ff, slots), BF16),
            jax.ShapeDtypeStruct((copies, groups, slots // groups), F32),
        ],
        [pltpu.VMEM((8, slots), F32)],
        2 * slots * ff * depth,
        2 * (ff + slots) * depth + 12 * ff * slots,
    )(where, gate, up, before, *args)


def down_kernel(counts, where_ref, here_ref, there_ref, *refs):
    at = 0
    for p, count in enumerate(counts):

        @pl.when((pl.program_id(0) >= at) & (pl.program_id(0) < at + count))
        def _(p=p):
            total = jnp.dot(here_ref[...], refs[2 * p][...], preferred_element_type=F32)
            total += jnp.dot(there_ref[...], refs[2 * p + 1][...], preferred_element_type=F32)
            refs[-1][...] = total.astype(BF16)

        at += count


def down(where, acts, pieces, width, into=None):
    half_ff, slots = acts[0].shape
    counts = [chunk[1] // TILE_D for _, _, chunk, _ in pieces]
    tiles = sum(counts)
    in_specs = [pl.BlockSpec((half_ff, slots), fixed)] * 2
    args = [where, *acts]
    starts = []
    for p, (here, there, _, _) in enumerate(pieces):
        start = sum(counts[:p])
        starts.append(start)
        place = lambda i, s, a=start, n=counts[p]: (0, jnp.clip(i - a, 0, n - 1))
        in_specs += [pl.BlockSpec((slots, TILE_D), place)] * 2
        args += [here, there]

    def place_out(i, s):
        at = 0
        for (_, _, chunk, side), start, count in zip(pieces, starts, counts):
            first = column(chunk, side)(s) * count
            at = jnp.where((i >= start) & (i < start + count), first + i - start, at)
        return (0, at)

    aliases = {}
    if into is not None:
        in_specs.append(pl.BlockSpec(memory_space=pl.ANY))
        aliases = {len(args): 0}
        args.append(into)
    return call(
        functools.partial(down_kernel, counts),
        "down",
        (tiles,),
        in_specs,
        pl.BlockSpec((half_ff, TILE_D), place_out),
        jax.ShapeDtypeStruct((half_ff, width), BF16),
        [],
        4 * half_ff * TILE_D * slots * tiles,
        2 * (half_ff * TILE_D + 2 * slots * TILE_D) * tiles + 4 * slots * half_ff,
        aliases,
    )(*args)


def combine_kernel(experts, route_ref, prob_ref, slot_ref, values_ref, out_ref):
    values = values_ref[0]
    for x in range(1, values_ref.shape[0]):
        values += values_ref[x]
    capacity = values.shape[1]
    tokens = route_ref.shape[1]
    columns = values.T
    place = lax.broadcasted_iota(jnp.int32, (capacity, tokens), 0).astype(F32)
    route = route_ref[...]
    total = jnp.zeros(route.shape, F32)
    for e in range(experts):
        hit = slot_ref[e : e + 1, :] == place
        mine = jnp.sum(jnp.where(hit, columns[:, e : e + 1], 0.0), axis=0, keepdims=True)
        total = jnp.where(route == e, mine, total)
    out_ref[...] = total / prob_ref[...].astype(F32)


def combine(route, prob, slot, values):
    experts = values.shape[1]
    return pl.pallas_call(
        functools.partial(combine_kernel, experts),
        out_shape=jax.ShapeDtypeStruct(route.shape, F32),
        name="combine",
    )(route, prob, slot, values)


def local(out_grad, route, gate_prob, w_down, gate_pre, up_pre):
    experts = lax.axis_size("expert")
    etp = lax.axis_size("etp")
    slots, ff = gate_pre.shape[1:]
    capacity = slots // experts
    width = out_grad.shape[1]
    parity = lax.bitwise_and(lax.axis_index("etp"), 1).reshape(1)
    where = jnp.concatenate([parity, parity, lax.axis_index("dp").reshape(1)])
    gate, up, w = gate_pre[0].T, up_pre[0].T, w_down[0]
    route, prob = route.T, gate_prob.T

    swap = [(2 * i, 2 * ((i - 1) % etp)) for i in range(etp)]
    swap += [(2 * i + 1, 2 * ((i + 1) % etp) + 1) for i in range(etp)]

    def fetch(send):
        x = send.reshape(experts, capacity, send.shape[1])
        x = lax.all_to_all(x, "expert", split_axis=0, concat_axis=0, tiled=True)
        return x.reshape(send.shape)

    def beside(x):
        return lax.ppermute(x, ("etp", "dp"), swap)

    def swap_dp(x):
        return lax.ppermute(x, "dp", [(0, 1), (1, 0)])

    c0, c1 = SHARED
    first, slot, pick = dispatch(parity, route, prob, out_grad, experts, capacity)
    gate, up, pick = lax.optimization_barrier((gate, up, pick))
    own0 = fetch(first)
    send1 = dispatch_more(parity, pick, out_grad, c1, OWN)
    send2 = dispatch_more(parity, pick, out_grad, DIRECT, SAME)
    act_other, act_mine = activation(where, gate, up)
    own0, send1, send2, act_other, act_mine = lax.optimization_barrier(
        (own0, send1, send2, act_other, act_mine)
    )
    acts = (act_mine, swap_dp(act_other))
    own1 = fetch(send1)
    oth0 = beside(own0)
    total = down(where, acts, [(own0, swap_dp(own0), c0, OWN)], width)
    total = down(where, acts, [(oth0, swap_dp(oth0), c0, OTHER)], width, total)
    own1, send2, total = lax.optimization_barrier((own1, send2, total))
    direct = fetch(send2)
    oth1 = beside(own1)
    raw = raw_part(where, w, [(own0, c0, OWN), (own1, c1, OWN), (oth0, c0, OTHER)])
    pieces = [(own1, swap_dp(own1), c1, OWN)]
    total = down(where, acts, pieces, width, total)
    direct, oth1, raw, total = lax.optimization_barrier((direct, oth1, raw, total))
    late = [(oth1, c1, OTHER), (direct, DIRECT, SAME)]
    grad_gate, grad_up, sums = finish(where, gate, up, raw, w, late, experts, etp)
    sums = sums.reshape(etp * experts, capacity)
    back = lax.all_to_all(sums, ("etp", "expert"), split_axis=0, concat_axis=0, tiled=True)
    pieces = [(rows, swap_dp(rows), chunk, side) for rows, chunk, side in late]
    total = down(where, acts, pieces, width, total)
    back, total = lax.optimization_barrier((back, total))
    grad_prob = combine(route, prob, slot, back.reshape(etp, experts, capacity))
    return grad_gate.T[None], grad_up.T[None], total[None], grad_prob.T


def solution(mesh):
    in_specs = (
        P(("expert", "dp"), None),
        P(("expert", "dp"), None),
        P(("expert", "dp"), None),
        P("expert", "etp", None),
        P("expert", "dp", "etp"),
        P("expert", "dp", "etp"),
    )
    out_specs = (
        P("expert", "dp", "etp"),
        P("expert", "dp", "etp"),
        P("expert", ("etp", "dp"), None),
        P(("expert", "dp"), None),
    )
    return jax.shard_map(local, mesh=mesh, in_specs=in_specs, out_specs=out_specs, check_vma=False)
```
